512 devices in a mesh: kpool: 16 (over z_hi, x, core), fft: 32 (over z_lo, y).
Axes of the slice: x: 4, y: 8, z: 8 (z_hi: 2, z_lo: 4; z = z_hi * 4 + z_lo), core: 2. Of those that a mesh axis runs over, the one named last changes fastest.
Arguments:
- coeff: bfloat16 [32, 2048, 1536], P('kpool', 'fft'), may hold values from -0.009765625 to 0.009765625
- col_map: int32 [32, 2048], P('kpool'), may hold values from 0 to 9215, as said below
- eigen: float32 [32, 2048], P('kpool'), may hold values from -2 to 2
- band_ids: int32 [8], replicated, may hold values from 0 to 2047, as said below
- tet_corners: int32 [192, 4], replicated, may hold values from 0 to 31, as said below
Outputs:
- density: float32 [192, 9216], P('fft', 'kpool')
The draws below stay inside these ranges and needn't reach their ends.
Inputs may be any that keep to these rules, and one draw needn't show every extreme that they name: `col_map`: each row holds 2048 distinct positions. `band_ids`: distinct bands. `tet_corners`: the four corners of a tetrahedron are distinct k-points, and every k-point is a corner of some tetrahedron.
All inputs are finite; a program needn't handle non-finite values.
Results may differ from the reference program's by a relative error of at most 0.0003.
The reference program's roundings to bfloat16 on the way count: a program that leaves them out, or rounds other values in their place, can miss the bound.
Values may be sent and summed in bfloat16 or wider, within the bound.
A program may use at most 64 MiB of HBM per device.

```python
import math
import jax
import jax.numpy as jnp
from jax import lax

NX = 96
NY = 96
NZ = 192
ZPW = 96
BANDS = 8
NB_ALL = 2048
COLS = 2048
KPOINTS = 32
NTET = 192


def choose_distinct(key, population, count):
    first_key, second_key = jax.random.split(key)
    middle = jax.random.permutation(first_key, jnp.arange(1, population - 1, dtype=jnp.int32))[:count - 2]
    chosen_values = jnp.concatenate([jnp.zeros((1,), jnp.int32), middle, jnp.full((1,), population - 1, jnp.int32)])
    shuffle_order = jax.random.permutation(second_key, jnp.arange(count, dtype=jnp.int32))
    return chosen_values[shuffle_order].astype(jnp.int32)


def draw_col_map(key, part):
    key = jax.random.fold_in(key, 11)
    kpoint_keys = jax.random.split(key, KPOINTS)

    def one_row(row_key):
        return choose_distinct(row_key, NX * NY, COLS)
    return jax.vmap(one_row)(kpoint_keys)


def draw_band_ids(key, part):
    key = jax.random.fold_in(key, 12)
    return choose_distinct(key, NB_ALL, BANDS)


def draw_tet_corners(key, part):
    key = jax.random.fold_in(key, 13)
    first_corner = jnp.arange(NTET, dtype=jnp.int32) % KPOINTS
    tetra_keys = jax.random.split(key, NTET)

    def one_tetra(tetra_key):
        return jax.random.permutation(tetra_key, jnp.arange(1, KPOINTS, dtype=jnp.int32))[:3]
    offsets = jax.vmap(one_tetra)(tetra_keys).astype(jnp.int32)
    others = (first_corner[:, None] + offsets) % KPOINTS
    return jnp.concatenate([first_corner[:, None], others], axis=1).astype(jnp.int32)


def level_of(key, shape, pieces, smallest, top_value):
    level = 1.0
    for dim, blocks in pieces:
        steps = jax.random.uniform(jax.random.fold_in(jax.random.fold_in(key, 6), dim), (blocks,), jnp.float32, smallest / len(pieces), top_value / len(pieces))
        level = level * jnp.repeat(jnp.exp(steps), shape[dim] // blocks).reshape((-1,) + (1,) * (len(shape) - 1 - dim))
    return level


def normal_values(rng, extent, scale, limit, pieces=(), kind=jnp.bfloat16):
    factor_of = level_of(rng, extent, pieces, -0.22, 0.18) if pieces else 1.0
    drawn = jax.random.normal(rng, extent, jnp.float32) * scale * factor_of
    return jnp.minimum(jnp.maximum(drawn, -limit), limit).astype(kind)


def setup_inputs(seed: int = 0) -> dict:
    arg_keys = jax.random.split(jax.random.key(seed), 6)
    coeff = normal_values(arg_keys[0], (KPOINTS, COLS, BANDS * 2 * ZPW), (2 * COLS * ZPW) ** -0.5, 0.009765625, ((0, 16), (1, 32)))
    col_map = draw_col_map(jax.random.fold_in(arg_keys[5], 71), 0)
    eigen = normal_values(arg_keys[2], (KPOINTS, NB_ALL), 0.3, 2.0, ((0, 16),), jnp.float32)
    band_ids = draw_band_ids(jax.random.fold_in(arg_keys[5], 71), 0)
    tet_corners = draw_tet_corners(jax.random.fold_in(arg_keys[5], 71), 0)
    return dict(coeff=coeff, col_map=col_map, eigen=eigen, band_ids=band_ids, tet_corners=tet_corners)


FERMI_LEVEL = 0.0
SMEARING = 0.1


def phase_table(frequencies, positions, period):
    product = (frequencies[:, None] % period) * positions[None, :] % period
    phases = (2.0 * math.pi / period) * product.astype(jnp.float32)
    cosine = jnp.cos(phases)
    sine_part = jnp.sin(phases)
    upper = jnp.stack([cosine, sine_part], axis=-1)
    lower = jnp.stack([-sine_part, cosine], axis=-1)
    return jnp.stack([upper, lower], axis=1).astype(jnp.bfloat16)


def tetra_weights(levels, corners):
    kpoint_count = levels.shape[0]
    tetra_count = corners.shape[0]
    corner_levels = levels[corners]
    mean_level = jnp.mean(corner_levels, axis=1)
    occupied = jax.nn.sigmoid((FERMI_LEVEL - mean_level) / SMEARING)
    repeated = jnp.repeat(occupied, 4, axis=0)
    onehot = (corners.reshape(-1)[:, None] == jnp.arange(kpoint_count, dtype=jnp.int32)[None, :]).astype(jnp.float32)
    summed = jnp.dot(onehot.T, repeated, precision=lax.Precision.HIGHEST)
    return summed * (2.0 / (4 * tetra_count))


def item_density(received, column_map, y_table, x_table):
    planes = received.shape[1] // 2
    dense_grid = jnp.zeros((received.shape[1], NX * NY), received.dtype).at[:, column_map].set(received.T)
    dense_grid = lax.optimization_barrier(dense_grid)
    dense_grid = dense_grid.reshape(planes, 2, NX, NY).astype(jnp.float32)
    along_y = jnp.einsum('pcxy,ycYC->pxCY', dense_grid, y_table.astype(jnp.float32)).astype(jnp.bfloat16)
    along_y = lax.optimization_barrier(along_y).astype(jnp.float32)
    along_x = jnp.einsum('pxCY,xCXD->pDXY', along_y, x_table.astype(jnp.float32))
    return jnp.sum(along_x * along_x, axis=1).reshape(planes, NX * NY)


def reference(coeff, col_map, eigen, band_ids, tet_corners):
    band_levels = jnp.take(eigen, band_ids, axis=1)
    weights = tetra_weights(band_levels, tet_corners)
    slots = jnp.arange(ZPW, dtype=jnp.int32) - ZPW // 2
    z_table = phase_table(slots, jnp.arange(NZ, dtype=jnp.int32), NZ).reshape(2 * ZPW, 2 * NZ)
    y_table = phase_table(jnp.arange(NY, dtype=jnp.int32), jnp.arange(NY, dtype=jnp.int32), NY)
    x_table = phase_table(jnp.arange(NX, dtype=jnp.int32), jnp.arange(NX, dtype=jnp.int32), NX)
    coeff_split = coeff.reshape(KPOINTS, COLS, BANDS, 2 * ZPW)

    def advance(running, position):
        kpoint = position // BANDS
        band = position % BANDS
        item_coeff = coeff_split[kpoint, :, band]
        columns = jnp.dot(item_coeff, z_table, preferred_element_type=jnp.float32).astype(jnp.bfloat16)
        term = item_density(columns, col_map[kpoint], y_table, x_table)
        return running + weights[kpoint, band] * term, None

    start = jnp.zeros((NZ, NX * NY), jnp.float32)
    density, unused = lax.scan(advance, start, jnp.arange(KPOINTS * BANDS, dtype=jnp.int32))
    return density
```

```python
import functools

import jax
import jax.numpy as jnp
import ml_dtypes
import numpy as np
from jax import lax
from jax.experimental import pallas as pl
from jax.experimental.pallas import tpu as pltpu
from jax.sharding import PartitionSpec as P

NX = 96
NY = 96
NZ = 192
ZPW = 96
BANDS = 8
COLS = 2048
KPOINTS = 32
NTET = 192

FFT = 32
POOLS = 16
KP = 2
LOCAL = COLS // FFT
PLANES = NZ // FFT
ROWS = 48
SMEARING = 0.1
MESH = pl.DeviceIdType.MESH
F32 = jnp.float32
BF16 = jnp.bfloat16
NT = (((1,), (1,)), ((), ()))


def phase_parts(frequencies, positions, period):
    product = frequencies[:, None] % period * positions[None, :] % period
    phases = np.float32(2.0 * np.pi / period) * product.astype(np.float32)
    return np.cos(phases), np.sin(phases)


def z_matrices():
    cosine, sine = phase_parts(np.arange(ZPW) - ZPW // 2, np.arange(NZ), NZ)
    full = np.zeros((ZPW, 2, NZ, 2), np.float32)
    full[:, 0, :, 0] = cosine
    full[:, 0, :, 1] = sine
    full[:, 1, :, 0] = -sine
    full[:, 1, :, 1] = cosine
    full = full.reshape(2 * ZPW, FFT, PLANES * 2).transpose(1, 2, 0)
    result = np.zeros((3, FFT, 8, 2, 2 * ZPW), np.float32)
    result[0, :, :, 0] = full[:, :8]
    result[1, :, :, 1] = full[:, :8]
    result[2, :, :4, 0] = full[:, 8:]
    result[2, :, 4:, 1] = full[:, 8:]
    return result.reshape(3, FFT * 8, 4 * ZPW).astype(ml_dtypes.bfloat16)


def y_matrix():
    cosine, sine = phase_parts(np.arange(NY), np.arange(NY), NY)
    result = np.zeros((2, 128, 2, 128), np.float32)
    result[0, :NY, 0, :NY] = cosine
    result[0, :NY, 1, :NY] = sine
    result[1, :NY, 0, :NY] = -sine
    result[1, :NY, 1, :NY] = cosine
    return result.reshape(256, 256).astype(ml_dtypes.bfloat16)


def x_matrix():
    cosine, sine = phase_parts(np.arange(NX), np.arange(NX), NX)
    result = np.zeros((2, 2, 4, 2, 8, 2, NX), np.float32)
    for core in range(2):
        for chip in range(4):
            for high in range(2):
                owner = (high * 4 + chip) * 2 + core
                mine = slice(owner * 6, owner * 6 + 6)
                result[0, core, chip, high, :6, 0] = cosine[:, mine].T
                result[0, core, chip, high, :6, 1] = -sine[:, mine].T
                result[1, core, chip, high, :6, 0] = sine[:, mine].T
                result[1, core, chip, high, :6, 1] = cosine[:, mine].T
    return result.reshape(256, 2 * NX).astype(ml_dtypes.bfloat16)


def iota(shape, dim):
    return lax.broadcasted_iota(jnp.int32, shape, dim).astype(F32)


def onehot(condition):
    return jnp.where(condition, 1.0, 0.0).astype(BF16)


def dot(a, b):
    return jnp.dot(a, b, preferred_element_type=F32)


def dot_nt(a, b):
    return lax.dot_general(a, b, NT, preferred_element_type=F32)


def wait_bytes(ref, sem):
    pltpu.make_async_copy(ref, ref, sem).wait()


def kernel(
    coeff, col_map, eigen, band_ids, corners, z_mat, y_mat, x_mat, out,
    send, recv, own_levels, levels, level_rows, weights, ranks, places, block_v, block_s,
    sorter, windows, columns, ordered, grid, density, half, in_core, in_x, in_z, quarter,
    send_sem, recv_sem, local_sem, level_sem, core_sem, x_send, x_recv, z_sem,
):
    fft = lax.axis_index("fft")
    pool = lax.axis_index("kpool")
    core = pool % 2
    chip = pool // 2 % 4
    high = pool // 8

    barrier = pltpu.get_barrier_semaphore()

    def greet_fft(step, carry):
        pl.semaphore_signal(
            barrier, inc=1, device_id={"fft": (fft + step) % FFT}, device_id_type=MESH
        )
        return carry

    def greet_pool(step, carry):
        pl.semaphore_signal(
            barrier, inc=1, device_id={"kpool": (pool + step) % POOLS}, device_id_type=MESH
        )
        return carry

    lax.fori_loop(1, FFT, greet_fft, 0)
    lax.fori_loop(1, POOLS, greet_pool, 0)

    def z_step(k):
        groups = []
        for pair in range(2):
            both = jnp.concatenate(
                [coeff[k, :, (2 * h + pair) * 384 : (2 * h + pair + 1) * 384] for h in range(2)],
                axis=0,
            )
            for part in range(3):
                groups.append(dot_nt(z_mat[part], both).reshape(FFT, 8, 128))
        for tile in range(3):
            joined = jnp.concatenate([groups[2 * tile], groups[2 * tile + 1]], axis=1)
            send[k, :, 16 * tile : 16 * tile + 16, :] = joined.astype(BF16)

    def send_columns(k):
        def one(step, carry):
            target = (fft + step) % FFT
            pltpu.make_async_remote_copy(
                src_ref=send.at[k, target],
                dst_ref=recv.at[k, fft],
                send_sem=send_sem.at[k],
                recv_sem=recv_sem.at[k],
                device_id={"fft": target},
                device_id_type=MESH,
            ).start()
            return carry

        lax.fori_loop(1, FFT, one, 0)
        pltpu.make_async_copy(send.at[k, fft], recv.at[k, fft], local_sem.at[k]).start()

    z_step(0)
    pl.semaphore_wait(barrier, FFT - 1 + POOLS - 1)
    send_columns(0)

    lanes = lax.broadcasted_iota(jnp.int32, (KP, 2048), 1)
    lane8 = lax.broadcasted_iota(jnp.int32, (KP, 128), 1)
    table = jnp.zeros((KP, 128), F32)
    for n in range(BANDS):
        picked = jnp.sum(jnp.where(lanes == band_ids[n], eigen[...], 0.0), axis=1, keepdims=True)
        table = jnp.where(lane8 == n, picked, table)
    own_levels[...] = jnp.zeros_like(own_levels)
    own_levels[0:KP, :] = table

    def send_levels(step, carry):
        pltpu.make_async_remote_copy(
            src_ref=own_levels,
            dst_ref=levels.at[pool],
            send_sem=level_sem.at[0],
            recv_sem=level_sem.at[1],
            device_id={"kpool": (pool + step) % POOLS},
            device_id_type=MESH,
        ).start()
        return carry

    lax.fori_loop(1, POOLS, send_levels, 0)
    pltpu.make_async_copy(own_levels, levels.at[pool], local_sem.at[2]).start()

    z_step(1)
    send_columns(1)

    for k in range(KP):
        place = col_map[k : k + 1, :].astype(F32)
        x_of = jnp.floor((place + 0.5) * (1.0 / NY))
        y_of = place - NY * x_of
        rows = iota((128, COLS), 0)
        in_x_row = rows == x_of
        x_hot = onehot(in_x_row)
        y_hot = onehot(rows == y_of)
        taken = dot_nt(x_hot, y_hot)
        first = iota((128, 128), 0)
        second = iota((128, 128), 1)
        taken_b = taken.astype(BF16)
        before = dot(taken_b, onehot(first < second))
        above = dot(onehot(second < first), taken_b)
        start = jnp.sum(above, axis=1, keepdims=True)
        x_from = lax.broadcasted_iota(jnp.int32, (NX, COLS), 0) * NY
        count = jnp.sum(
            jnp.where(col_map[k : k + 1, :] < x_from, 1, 0), axis=1, keepdims=True
        )
        block_v[k] = jnp.broadcast_to(jnp.minimum(count >> 7, COLS // 128 - 1), (NX, 128))
        block = jnp.minimum(jnp.floor(start * (1.0 / 128)), COLS // 128 - 1.0)
        places[k] = jnp.where(taken > 0.5, start + before - 128.0 * block, -1.0)
        within = dot(before.astype(BF16), y_hot)
        ranks[k : k + 1, :] = jnp.sum(
            jnp.where(in_x_row, start + within, 0.0), axis=0, keepdims=True
        )
    block_copy = pltpu.make_async_copy(block_v, block_s, local_sem.at[3])
    block_copy.start()

    for k in range(KP):
        def sorter_rows(step, carry, k=k):
            at = pl.multiple_of(step * 64, 64)
            rows = iota((64, COLS), 0) + (step * 64).astype(F32)
            sorter[k, pl.ds(at, 64), :] = onehot(rows == ranks[k : k + 1, :])
            return carry

        lax.fori_loop(0, COLS // 64, sorter_rows, 0)

        def window(x, carry, k=k):
            windows[k, x] = onehot(iota((256, 128), 0) == places[k, pl.ds(x, 1), :])
            return carry

        lax.fori_loop(0, NX, window, 0)

    wait_bytes(levels.at[pl.ds(0, POOLS - 1)], level_sem.at[1])
    pltpu.make_async_copy(own_levels, levels.at[pool], local_sem.at[2]).wait()
    level_rows[...] = jnp.zeros_like(level_rows)
    for j in range(POOLS):
        level_rows[KP * j : KP * j + KP, :] = levels[j, 0:KP, :]
    kpoint = lax.broadcasted_iota(jnp.int32, (NTET, 128), 1)
    member = jnp.zeros((NTET, 128), F32)
    for c in range(4):
        member = member + jnp.where(corners[:, c : c + 1] == kpoint, 1.0, 0.0)
    mean = 0.25 * jnp.dot(
        member, level_rows[...], precision=lax.Precision.HIGHEST, preferred_element_type=F32
    )
    occupied = jax.nn.sigmoid((0.0 - mean) / SMEARING)
    lane128 = lax.broadcasted_iota(jnp.int32, (1, 128), 1)
    for k in range(KP):
        mine = jnp.sum(
            jnp.where(kpoint == pool * KP + k, member, 0.0), axis=1, keepdims=True
        )
        row = jnp.sum(mine * occupied, axis=0, keepdims=True) * (2.0 / (4 * NTET))
        for n in range(BANDS):
            value = jnp.sum(jnp.where(lane128 == n, row, 0.0), axis=1, keepdims=True)
            weights[k * BANDS + n : k * BANDS + n + 1, :] = jnp.broadcast_to(value, (1, 128))

    ordered[COLS // 128] = jnp.zeros((2 * ROWS, 128), BF16)
    density[...] = jnp.zeros_like(density)
    block_copy.wait()

    for k in range(KP):
        wait_bytes(recv.at[k, pl.ds(0, FFT - 1)], recv_sem.at[k])
        pltpu.make_async_copy(send.at[k, fft], recv.at[k, fft], local_sem.at[k]).wait()

        def merge(step, carry, k=k):
            even = recv[k, 2 * step].astype(F32)
            odd = recv[k, 2 * step + 1].astype(F32)
            low = lax.broadcasted_iota(jnp.int32, (ROWS, 128), 1) < LOCAL
            at = pl.ds(pl.multiple_of(step * 128, 128), 128)
            columns[0:ROWS, at] = jnp.where(low, even, pltpu.roll(odd, LOCAL, 1)).astype(BF16)
            columns[ROWS:, at] = jnp.where(low, pltpu.roll(even, LOCAL, 1), odd).astype(BF16)
            return carry

        lax.fori_loop(0, FFT // 2, merge, 0, unroll=4)

        def order(step, carry, k=k):
            at = pl.ds(pl.multiple_of(step * 256, 256), 256)
            part = dot_nt(columns[...], sorter[k, at, :]).astype(BF16)
            ordered[2 * step] = part[:, :128]
            ordered[2 * step + 1] = part[:, 128:]
            return carry

        lax.fori_loop(0, COLS // 256, order, 0, unroll=2)

        def grid_row(x, carry, k=k):
            block = block_s[k, x, 0]
            near = jnp.concatenate([ordered[block], ordered[block + 1]], axis=1)
            grid[pl.ds(pl.multiple_of(x * 2 * ROWS, 8), 2 * ROWS), :] = dot(near, windows[k, x])
            return carry

        lax.fori_loop(0, NX, grid_row, 0, unroll=8)

        def band_pair(step, carry, k=k):
            weight = [
                weights[pl.ds(k * BANDS + 2 * step + e, 1), :] for e in range(2)
            ]
            for p in range(PLANES):
                row = step * 24 + (2 * p if p < 4 else 16 + 2 * (p - 4))
                apart = 8 if p < 4 else 4
                field = jnp.concatenate(
                    [
                        jnp.concatenate(
                            [
                                grid[pl.ds(row + apart * e + c, NX, stride=2 * ROWS), :]
                                for c in range(2)
                            ],
                            axis=1,
                        )
                        for e in range(2)
                    ],
                    axis=0,
                ).astype(BF16)
                along_y = dot(field, y_mat[...]).astype(BF16)
                turned = jnp.concatenate(
                    [
                        jnp.concatenate([along_y[:NX, :128], along_y[NX:, :128]], axis=1),
                        jnp.concatenate([along_y[:NX, 128:], along_y[NX:, 128:]], axis=1),
                    ],
                    axis=0,
                )
                psi = dot(x_mat[...], turned)
                power = psi[:128] * psi[:128] + psi[128:] * psi[128:]
                density[p] += weight[0] * power[:, :128] + weight[1] * power[:, 128:]
            return carry

        lax.fori_loop(0, BANDS // 2, band_pair, 0)

    other = pl.ds(pl.multiple_of((1 - core) * 64, 64), 64)
    mine = pl.ds(pl.multiple_of(core * 64, 64), 64)
    core_copy = pltpu.make_async_remote_copy(
        src_ref=density.at[:, other, :],
        dst_ref=in_core,
        send_sem=core_sem.at[0],
        recv_sem=core_sem.at[1],
        device_id={"kpool": pool + 1 - 2 * core},
        device_id_type=MESH,
    )
    core_copy.start()
    core_copy.wait()
    half[...] = density[:, mine, :] + in_core[...]
    x_copies = []
    for step in range(1, 4):
        target = (chip + step) % 4
        copy = pltpu.make_async_remote_copy(
            src_ref=half.at[:, pl.ds(pl.multiple_of(target * 16, 16), 16), :],
            dst_ref=in_x.at[step - 1],
            send_sem=x_send.at[step - 1],
            recv_sem=x_recv.at[step - 1],
            device_id={"kpool": (high * 4 + target) * 2 + core},
            device_id_type=MESH,
        )
        copy.start()
        x_copies.append(copy)
    for copy in x_copies:
        copy.wait()
    quarter[...] = (
        half[:, pl.ds(pl.multiple_of(chip * 16, 16), 16), :] + in_x[0] + in_x[1] + in_x[2]
    )
    z_copy = pltpu.make_async_remote_copy(
        src_ref=quarter.at[:, pl.ds(pl.multiple_of((1 - high) * 8, 8), 8), :],
        dst_ref=in_z,
        send_sem=z_sem.at[0],
        recv_sem=z_sem.at[1],
        device_id={"kpool": pool + 8 - 16 * high},
        device_id_type=MESH,
    )
    z_copy.start()
    z_copy.wait()
    total = quarter[:, pl.ds(pl.multiple_of(high * 8, 8), 8), :] + in_z[...]
    for i in range(6):
        out[:, NY * i : NY * (i + 1)] = total[:, i, :NY]

    for k in range(KP):
        wait_bytes(send.at[k, pl.ds(0, FFT - 1)], send_sem.at[k])
    wait_bytes(levels.at[pl.ds(0, POOLS - 1)], level_sem.at[0])


def per_device(coeff, col_map, eigen, band_ids, tet_corners):
    vmem = pl.BlockSpec(memory_space=pltpu.VMEM)
    smem = pl.BlockSpec(memory_space=pltpu.SMEM)
    return pl.pallas_call(
        kernel,
        out_shape=jax.ShapeDtypeStruct((PLANES, 6 * NY), F32),
        in_specs=[vmem, vmem, vmem, smem, vmem, vmem, vmem, vmem],
        out_specs=vmem,
        scratch_shapes=[
            pltpu.VMEM((KP, FFT, ROWS, 128), BF16),
            pltpu.VMEM((KP, FFT, ROWS, 128), BF16),
            pltpu.VMEM((8, 128), F32),
            pltpu.VMEM((POOLS, 8, 128), F32),
            pltpu.VMEM((128, 128), F32),
            pltpu.VMEM((KP * BANDS, 128), F32),
            pltpu.VMEM((8, COLS), F32),
            pltpu.VMEM((KP, 128, 128), F32),
            pltpu.VMEM((KP, NX, 128), jnp.int32),
            pltpu.SMEM((KP, NX, 128), jnp.int32),
            pltpu.VMEM((KP, COLS, COLS), BF16),
            pltpu.VMEM((KP, NX, 256, 128), BF16),
            pltpu.VMEM((2 * ROWS, COLS), BF16),
            pltpu.VMEM((COLS // 128 + 1, 2 * ROWS, 128), BF16),
            pltpu.VMEM((NX * 2 * ROWS, 128), F32),
            pltpu.VMEM((PLANES, 128, 128), F32),
            pltpu.VMEM((PLANES, 64, 128), F32),
            pltpu.VMEM((PLANES, 64, 128), F32),
            pltpu.VMEM((3, PLANES, 16, 128), F32),
            pltpu.VMEM((PLANES, 8, 128), F32),
            pltpu.VMEM((PLANES, 16, 128), F32),
            pltpu.SemaphoreType.DMA((KP,)),
            pltpu.SemaphoreType.DMA((KP,)),
            pltpu.SemaphoreType.DMA((4,)),
            pltpu.SemaphoreType.DMA((2,)),
            pltpu.SemaphoreType.DMA((2,)),
            pltpu.SemaphoreType.DMA((3,)),
            pltpu.SemaphoreType.DMA((3,)),
            pltpu.SemaphoreType.DMA((2,)),
        ],
        compiler_params=pltpu.CompilerParams(
            collective_id=0, has_side_effects=True, vmem_limit_bytes=56 * 1024 * 1024
        ),
    )(
        coeff, col_map, eigen, band_ids, tet_corners,
        jnp.asarray(z_matrices()), jnp.asarray(y_matrix()), jnp.asarray(x_matrix()),
    )


def solution(mesh):
    in_specs = (P("kpool", "fft", None), P("kpool", None), P("kpool", None), P(), P())
    out_specs = P("fft", "kpool")
    return jax.shard_map(
        per_device, mesh=mesh, in_specs=in_specs, out_specs=out_specs, check_vma=False
    )
```

```python
import functools

import jax
import jax.numpy as jnp
import ml_dtypes
import numpy as np
from jax import lax
from jax.experimental import pallas as pl
from jax.experimental.pallas import tpu as pltpu
from jax.sharding import PartitionSpec as P

NX = 96
NY = 96
NZ = 192
ZPW = 96
BANDS = 8
COLS = 2048
KPOINTS = 32
NTET = 192

FFT = 32
POOLS = 16
KP = 2
LOCAL = COLS // FFT
PLANES = NZ // FFT
ROWS = 48
GROUP = 4
GROUPS = FFT // GROUP
WIDE = GROUP * LOCAL
PITCH = 2 * ROWS + 8
BATCH = 2
BATCHES = PLANES // BATCH
SMEARING = 0.1
MESH = pl.DeviceIdType.MESH
F32 = jnp.float32
BF16 = jnp.bfloat16
NT = (((1,), (1,)), ((), ()))


def phase_parts(frequencies, positions, period):
    product = frequencies[:, None] % period * positions[None, :] % period
    phases = np.float32(2.0 * np.pi / period) * product.astype(np.float32)
    return np.cos(phases), np.sin(phases)


def z_matrices():
    cosine, sine = phase_parts(np.arange(ZPW) - ZPW // 2, np.arange(NZ), NZ)
    full = np.zeros((ZPW, 2, NZ, 2), np.float32)
    full[:, 0, :, 0] = cosine
    full[:, 0, :, 1] = sine
    full[:, 1, :, 0] = -sine
    full[:, 1, :, 1] = cosine
    full = full.reshape(2 * ZPW, FFT, PLANES * 2).transpose(1, 2, 0)
    result = np.zeros((3, FFT, 8, 2, 2 * ZPW), np.float32)
    result[0, :, :, 0] = full[:, :8]
    result[1, :, :, 1] = full[:, :8]
    result[2, :, :4, 0] = full[:, 8:]
    result[2, :, 4:, 1] = full[:, 8:]
    return result.reshape(3 * FFT * 8, 4 * ZPW).astype(ml_dtypes.bfloat16)


def y_matrix():
    cosine, sine = phase_parts(np.arange(NY), np.arange(NY), NY)
    result = np.zeros((2, 128, 2, 128), np.float32)
    result[0, :NY, 0, :NY] = cosine
    result[0, :NY, 1, :NY] = sine
    result[1, :NY, 0, :NY] = -sine
    result[1, :NY, 1, :NY] = cosine
    return result.reshape(256, 256).astype(ml_dtypes.bfloat16)


def x_matrix():
    cosine, sine = phase_parts(np.arange(NX), np.arange(NX), NX)
    result = np.zeros((2, 2, 4, 2, 8, 2, NX), np.float32)
    for core in range(2):
        for chip in range(4):
            for high in range(2):
                owner = (high * 4 + chip) * 2 + core
                mine = slice(owner * 6, owner * 6 + 6)
                result[0, core, chip, high, :6, 0] = cosine[:, mine].T
                result[0, core, chip, high, :6, 1] = -sine[:, mine].T
                result[1, core, chip, high, :6, 0] = sine[:, mine].T
                result[1, core, chip, high, :6, 1] = cosine[:, mine].T
    return result.reshape(256, 2 * NX).astype(ml_dtypes.bfloat16)


def iota(shape, dim):
    return lax.broadcasted_iota(jnp.int32, shape, dim).astype(F32)


def onehot(condition):
    return jnp.where(condition, 1.0, 0.0).astype(BF16)


def dot(a, b):
    return jnp.dot(a, b, preferred_element_type=F32)


def dot_nt(a, b):
    return lax.dot_general(a, b, NT, preferred_element_type=F32)


def wait_bytes(ref, sem):
    pltpu.make_async_copy(ref, ref, sem).wait()


def kernel(
    coeff, col_map, eigen, band_ids, corners, z_mat, y_mat, x_mat, out,
    send, recv, own_levels, levels, weights, ranks, places, block_v, block_s,
    sorter, windows, columns, ordered, ordered_b, grid, field, density,
    in_core, half, in_x, quarter, in_z,
    send_sem, recv_sem, local_sem, level_sem, core_sem, x_sem, z_sem,
):
    fft = lax.axis_index("fft")
    pool = lax.axis_index("kpool")
    core = pool % 2
    chip = pool // 2 % 4
    high = pool // 8

    barrier = pltpu.get_barrier_semaphore()

    def greet_fft(step, carry):
        pl.semaphore_signal(
            barrier, inc=1, device_id={"fft": (fft + step) % FFT}, device_id_type=MESH
        )
        return carry

    def greet_pool(step, carry):
        pl.semaphore_signal(
            barrier, inc=1, device_id={"kpool": (pool + step) % POOLS}, device_id_type=MESH
        )
        return carry

    lax.fori_loop(1, FFT, greet_fft, 0)
    lax.fori_loop(1, POOLS, greet_pool, 0)

    def z_step(k):
        groups = []
        for pair in range(2):
            both = jnp.concatenate(
                [coeff[k, :, (2 * h + pair) * 384 : (2 * h + pair + 1) * 384] for h in range(2)],
                axis=0,
            )
            parts = dot_nt(z_mat[...], both).reshape(3, FFT, 8, 128)
            groups.extend(parts[part] for part in range(3))
        for tile in range(3):
            joined = jnp.concatenate([groups[2 * tile], groups[2 * tile + 1]], axis=1)
            send[k, :, 16 * tile : 16 * tile + 16, :] = joined.astype(BF16)

    def send_columns(k):
        def one(step, carry):
            target = (fft + step) % FFT
            pltpu.make_async_remote_copy(
                src_ref=send.at[k, target],
                dst_ref=recv.at[k, fft],
                send_sem=send_sem.at[k],
                recv_sem=recv_sem.at[k, fft // GROUP],
                device_id={"fft": target},
                device_id_type=MESH,
            ).start()
            return carry

        lax.fori_loop(1, FFT, one, 0)
        pltpu.make_async_copy(send.at[k, fft], recv.at[k, fft], local_sem.at[k]).start()

    z_step(0)
    pl.semaphore_wait(barrier, FFT - 1 + POOLS - 1)
    send_columns(0)

    band = lax.broadcasted_iota(jnp.int32, (BANDS, 2048), 0)
    chosen = jnp.zeros((BANDS, 2048), jnp.int32)
    for n in range(BANDS):
        chosen = jnp.where(band == n, band_ids[n], chosen)
    found = chosen == lax.broadcasted_iota(jnp.int32, (BANDS, 2048), 1)
    lane = lax.broadcasted_iota(jnp.int32, (BANDS, 128), 1)
    table = jnp.zeros((BANDS, 128), F32)
    for k in range(KP):
        picked = jnp.sum(jnp.where(found, eigen[k : k + 1, :], 0.0), axis=1, keepdims=True)
        table = jnp.where(lane == pool * KP + k, picked, table)
    own_levels[...] = table

    def send_levels(step, carry):
        pltpu.make_async_remote_copy(
            src_ref=own_levels,
            dst_ref=levels.at[pool],
            send_sem=level_sem.at[0],
            recv_sem=level_sem.at[1],
            device_id={"kpool": (pool + step) % POOLS},
            device_id_type=MESH,
        ).start()
        return carry

    lax.fori_loop(1, POOLS, send_levels, 0)
    pltpu.make_async_copy(own_levels, levels.at[pool], local_sem.at[2]).start()

    z_step(1)

    for k in range(KP):
        place = col_map[k : k + 1, :].astype(F32)
        x_of = jnp.floor((place + 0.5) * (1.0 / NY))
        y_of = place - NY * x_of
        rows = iota((128, COLS), 0)
        in_x_row = rows == x_of
        x_hot = onehot(in_x_row)
        y_hot = onehot(rows == y_of)
        taken = dot_nt(x_hot, y_hot)
        first = iota((128, 128), 0)
        second = iota((128, 128), 1)
        taken_b = taken.astype(BF16)
        before = dot(taken_b, onehot(first < second))
        above = dot(onehot(second < first), taken_b)
        start = jnp.sum(above, axis=1, keepdims=True)
        x_from = lax.broadcasted_iota(jnp.int32, (NX, COLS), 0) * NY
        count = jnp.sum(
            jnp.where(col_map[k : k + 1, :] < x_from, 1, 0), axis=1, keepdims=True
        )
        block_v[k] = jnp.broadcast_to(jnp.minimum(count >> 7, COLS // 128 - 1), (NX, 128))
        block = jnp.minimum(jnp.floor(start * (1.0 / 128)), COLS // 128 - 1.0)
        places[k] = jnp.where(taken > 0.5, start + before - 128.0 * block, -1.0).astype(jnp.int32)
        within = dot(before.astype(BF16), y_hot)
        rank = jnp.sum(jnp.where(in_x_row, start + within, 0.0), axis=0, keepdims=True)
        for group in range(GROUPS):
            ranks[k, group : group + 1, :] = rank[:, WIDE * group : WIDE * (group + 1)]
    block_copy = pltpu.make_async_copy(block_v, block_s, local_sem.at[3])
    block_copy.start()

    for k in range(KP):
        def sorter_rows(step, carry, k=k):
            group = step // 8
            part = step % 8
            rows = lax.broadcasted_iota(jnp.int32, (256, WIDE), 0) + part * 256
            sorter[
                k,
                pl.ds(pl.multiple_of(part * 256, 256), 256),
                pl.ds(pl.multiple_of(group * WIDE, WIDE), WIDE),
            ] = onehot(rows.astype(F32) == ranks[k, pl.ds(group, 1), :])
            return carry

        lax.fori_loop(0, GROUPS * 8, sorter_rows, 0)

        def window(step, carry, k=k):
            windows[k, step] = onehot(
                lax.broadcasted_iota(jnp.int32, (256, 128), 0)
                == places[k, pl.ds(2 * step + 1, 1), :]
            )
            return carry

        lax.fori_loop(0, NX // 2, window, 0)

    wait_bytes(send.at[0, pl.ds(0, FFT - 1)], send_sem.at[0])
    send_columns(1)

    def find_weights():
        wait_bytes(levels.at[pl.ds(0, POOLS - 1)], level_sem.at[1])
        pltpu.make_async_copy(own_levels, levels.at[pool], local_sem.at[2]).wait()
        every = levels[0]
        for j in range(1, POOLS):
            every = every + levels[j]
        kpoint = lax.broadcasted_iota(jnp.int32, (128, NTET), 0)
        member = jnp.zeros((128, NTET), F32)
        for c in range(4):
            member = member + jnp.where(corners[c : c + 1, :] == kpoint, 1.0, 0.0)
        mean = 0.25 * jnp.dot(
            every, member, precision=lax.Precision.HIGHEST, preferred_element_type=F32
        )
        occupied = jax.nn.sigmoid((0.0 - mean) / SMEARING)
        for k in range(KP):
            mine = jnp.zeros((1, NTET), F32)
            for c in range(4):
                mine = mine + jnp.where(corners[c : c + 1, :] == pool * KP + k, 1.0, 0.0)
            weight = jnp.sum(mine * occupied, axis=1, keepdims=True) * (2.0 / (4 * NTET))
            weights[k * BANDS : (k + 1) * BANDS, :] = jnp.broadcast_to(weight, (BANDS, 128))

    low = lax.broadcasted_iota(jnp.int32, (ROWS, 128), 1) < LOCAL

    def gather_group(k, group):
        upper, lower = [], []
        for pair in range(GROUP // 2):
            even = recv[k, GROUP * group + 2 * pair].astype(F32)
            odd = recv[k, GROUP * group + 2 * pair + 1].astype(F32)
            upper.append(jnp.where(low, even, pltpu.roll(odd, LOCAL, 1)))
            lower.append(jnp.where(low, pltpu.roll(even, LOCAL, 1), odd))
        return jnp.concatenate(
            [jnp.concatenate(upper, axis=1), jnp.concatenate(lower, axis=1)], axis=0
        ).astype(BF16)

    def each_group(k, work):
        def one(step, carry):
            group = (fft // GROUP + GROUPS - step) % GROUPS
            wait_bytes(recv.at[k, pl.ds(0, GROUP)], recv_sem.at[k, group])
            work(group)
            return carry

        lax.fori_loop(1, GROUPS, one, 0)
        group = fft // GROUP
        wait_bytes(recv.at[k, pl.ds(0, GROUP - 1)], recv_sem.at[k, group])
        pltpu.make_async_copy(send.at[k, fft], recv.at[k, fft], local_sem.at[k]).wait()
        work(group)

    def order_as_they_come(k):
        ordered[...] = jnp.zeros_like(ordered)

        def work(group):
            part_columns = gather_group(k, group)
            at = pl.ds(pl.multiple_of(group * WIDE, WIDE), WIDE)
            for part in range(8):
                moved = dot_nt(part_columns, sorter[k, 256 * part : 256 * (part + 1), at])
                ordered[2 * part] += moved[:, :128]
                ordered[2 * part + 1] += moved[:, 128:]

        each_group(k, work)

    def order_at_once(k):
        def work(group):
            columns[:, pl.ds(pl.multiple_of(group * WIDE, WIDE), WIDE)] = gather_group(k, group)

        each_group(k, work)

        def chunk(step, carry):
            at = pl.ds(pl.multiple_of(step * 256, 256), 256)
            moved = dot_nt(columns[...], sorter[k, at, :])
            ordered[2 * step] = moved[:, :128]
            ordered[2 * step + 1] = moved[:, 128:]
            return carry

        lax.fori_loop(0, COLS // 256, chunk, 0, unroll=2)

    def fill_grid(k):
        for block in range(COLS // 128 + 1):
            ordered_b[block] = ordered[block].astype(BF16)

        def two(step, carry):
            x = 2 * step
            block = block_s[k, x, 0]
            place = jnp.broadcast_to(places[k, pl.ds(x, 1), :], (2 * ROWS, 128))
            lane = place & 127
            near = jnp.take_along_axis(ordered[block], lane, axis=1, mode="promise_in_bounds")
            far = jnp.take_along_axis(ordered[block + 1], lane, axis=1, mode="promise_in_bounds")
            row = jnp.where(place < 0, 0.0, jnp.where(place < 128, near, far))
            grid[pl.ds(x * PITCH, 2 * ROWS), :] = row
            block = block_s[k, x + 1, 0]
            both = jnp.concatenate([ordered_b[block], ordered_b[block + 1]], axis=1)
            grid[pl.ds(x * PITCH + PITCH, 2 * ROWS), :] = dot(both, windows[k, step])
            return carry

        lax.fori_loop(0, NX // 2, two, 0, unroll=4)

    def add_plane(k, p):
        for pair in range(BANDS // 2):
            row = pair * 24 + (2 * p if p < 4 else 16 + 2 * (p - 4))
            apart = 8 if p < 4 else 4
            for e in range(2):
                for c in range(2):
                    field[(2 * pair + e) * NX : (2 * pair + e + 1) * NX, 128 * c : 128 * (c + 1)] = (
                        grid[pl.ds(row + apart * e + c, NX, stride=PITCH), :].astype(BF16)
                    )
        along_y = dot(field[...], y_mat[...]).astype(BF16)
        total = density[p]
        for pair in range(BANDS // 2):
            one, two = (
                along_y[(2 * pair + e) * NX : (2 * pair + e + 1) * NX] for e in range(2)
            )
            turned = jnp.concatenate(
                [
                    jnp.concatenate([one[:, :128], two[:, :128]], axis=1),
                    jnp.concatenate([one[:, 128:], two[:, 128:]], axis=1),
                ],
                axis=0,
            )
            psi = dot(x_mat[...], turned)
            power = psi[:128] * psi[:128] + psi[128:] * psi[128:]
            at = k * BANDS + 2 * pair
            total = total + (
                weights[at : at + 1, :] * power[:, :128]
                + weights[at + 1 : at + 2, :] * power[:, 128:]
            )
        density[p] = total

    def planes(batch):
        return pl.ds(BATCH * batch, BATCH)

    def rows_of(index, size):
        return pl.ds(pl.multiple_of(index * size, size), size)

    def core_copy(batch):
        return pltpu.make_async_remote_copy(
            src_ref=density.at[planes(batch), rows_of(1 - core, 64), :],
            dst_ref=in_core.at[planes(batch)],
            send_sem=core_sem.at[0, batch],
            recv_sem=core_sem.at[1, batch],
            device_id={"kpool": pool + 1 - 2 * core},
            device_id_type=MESH,
        )

    def x_copies(batch):
        copies = []
        for step in range(1, 4):
            target = (chip + step) % 4
            copies.append(
                pltpu.make_async_remote_copy(
                    src_ref=half.at[planes(batch), rows_of(target, 16), :],
                    dst_ref=in_x.at[step - 1, planes(batch)],
                    send_sem=x_sem.at[0, step - 1, batch],
                    recv_sem=x_sem.at[1, step - 1, batch],
                    device_id={"kpool": (high * 4 + target) * 2 + core},
                    device_id_type=MESH,
                )
            )
        return copies

    def z_copy(batch):
        return pltpu.make_async_remote_copy(
            src_ref=quarter.at[planes(batch), rows_of(1 - high, 8), :],
            dst_ref=in_z.at[planes(batch)],
            send_sem=z_sem.at[0, batch],
            recv_sem=z_sem.at[1, batch],
            device_id={"kpool": pool + 8 - 16 * high},
            device_id_type=MESH,
        )

    def sum_core(batch):
        core_copy(batch).wait_recv()
        at = planes(batch)
        half[at] = density[at, rows_of(core, 64), :] + in_core[at]
        for copy in x_copies(batch):
            copy.start()

    def sum_x(batch):
        at = planes(batch)
        total = half[at, rows_of(chip, 16), :]
        for step, copy in enumerate(x_copies(batch)):
            copy.wait_recv()
            total = total + in_x[step, at]
        quarter[at] = total
        z_copy(batch).start()

    def sum_z(batch):
        z_copy(batch).wait_recv()
        at = planes(batch)
        total = quarter[at, rows_of(high, 8), :] + in_z[at]
        for i in range(6):
            out[BATCH * batch : BATCH * (batch + 1), NY * i : NY * (i + 1)] = total[:, i, :NY]

    density[...] = jnp.zeros_like(density)
    block_copy.wait()

    order_as_they_come(0)
    find_weights()
    fill_grid(0)
    for p in range(PLANES):
        add_plane(0, p)
    order_at_once(1)
    fill_grid(1)
    for step in range(BATCHES + 2):
        if step < BATCHES:
            for p in range(BATCH):
                add_plane(1, BATCH * step + p)
            core_copy(step).start()
        if 1 <= step <= BATCHES:
            sum_core(step - 1)
        if step >= 2:
            sum_x(step - 2)
    for batch in range(BATCHES):
        sum_z(batch)

    for batch in range(BATCHES):
        core_copy(batch).wait_send()
        for copy in x_copies(batch):
            copy.wait_send()
        z_copy(batch).wait_send()
    wait_bytes(send.at[1, pl.ds(0, FFT - 1)], send_sem.at[1])
    wait_bytes(levels.at[pl.ds(0, POOLS - 1)], level_sem.at[0])


def per_device(coeff, col_map, eigen, band_ids, tet_corners):
    vmem = pl.BlockSpec(memory_space=pltpu.VMEM)
    smem = pl.BlockSpec(memory_space=pltpu.SMEM)
    return pl.pallas_call(
        kernel,
        out_shape=jax.ShapeDtypeStruct((PLANES, 6 * NY), F32),
        in_specs=[vmem, vmem, vmem, smem, vmem, vmem, vmem, vmem],
        out_specs=vmem,
        scratch_shapes=[
            pltpu.VMEM((KP, FFT, ROWS, 128), BF16),
            pltpu.VMEM((KP, FFT, ROWS, 128), BF16),
            pltpu.VMEM((8, 128), F32),
            pltpu.VMEM((POOLS, 8, 128), F32),
            pltpu.VMEM((KP * BANDS, 128), F32),
            pltpu.VMEM((KP, GROUPS, WIDE), F32),
            pltpu.VMEM((KP, 128, 128), jnp.int32),
            pltpu.VMEM((KP, NX, 128), jnp.int32),
            pltpu.SMEM((KP, NX, 128), jnp.int32),
            pltpu.VMEM((KP, COLS, COLS), BF16),
            pltpu.VMEM((KP, NX // 2, 256, 128), BF16),
            pltpu.VMEM((2 * ROWS, COLS), BF16),
            pltpu.VMEM((COLS // 128 + 1, 2 * ROWS, 128), F32),
            pltpu.VMEM((COLS // 128 + 1, 2 * ROWS, 128), BF16),
            pltpu.VMEM((NX * PITCH, 128), F32),
            pltpu.VMEM((BANDS * NX, 256), BF16),
            pltpu.VMEM((PLANES, 128, 128), F32),
            pltpu.VMEM((PLANES, 64, 128), F32),
            pltpu.VMEM((PLANES, 64, 128), F32),
            pltpu.VMEM((3, PLANES, 16, 128), F32),
            pltpu.VMEM((PLANES, 16, 128), F32),
            pltpu.VMEM((PLANES, 8, 128), F32),
            pltpu.SemaphoreType.DMA((KP,)),
            pltpu.SemaphoreType.DMA((KP, GROUPS)),
            pltpu.SemaphoreType.DMA((4,)),
            pltpu.SemaphoreType.DMA((2,)),
            pltpu.SemaphoreType.DMA((2, BATCHES)),
            pltpu.SemaphoreType.DMA((2, 3, BATCHES)),
            pltpu.SemaphoreType.DMA((2, BATCHES)),
        ],
        compiler_params=pltpu.CompilerParams(
            collective_id=0, has_side_effects=True, vmem_limit_bytes=56 * 1024 * 1024
        ),
    )(
        coeff, col_map, eigen, band_ids, tet_corners.T,
        jnp.asarray(z_matrices()), jnp.asarray(y_matrix()), jnp.asarray(x_matrix()),
    )


def solution(mesh):
    in_specs = (P("kpool", "fft", None), P("kpool", None), P("kpool", None), P(), P())
    out_specs = P("fft", "kpool")
    return jax.shard_map(
        per_device, mesh=mesh, in_specs=in_specs, out_specs=out_specs, check_vma=False
    )
```

```python
import functools

import jax
import jax.numpy as jnp
import ml_dtypes
import numpy as np
from jax import lax
from jax.experimental import pallas as pl
from jax.experimental.pallas import tpu as pltpu
from jax.sharding import PartitionSpec as P

NX = 96
NY = 96
NZ = 192
ZPW = 96
BANDS = 8
COLS = 2048
KPOINTS = 32
NTET = 192

FFT = 32
POOLS = 16
KP = 2
LOCAL = COLS // FFT
PLANES = NZ // FFT
ROWS = 48
GROUP = 4
GROUPS = FFT // GROUP
WIDE = GROUP * LOCAL
PITCH = 2 * ROWS + 8
BATCH = 2
OWNED = 6
BATCHES = PLANES // BATCH
SMEARING = 0.1
MESH = pl.DeviceIdType.MESH
F32 = jnp.float32
BF16 = jnp.bfloat16
NT = (((1,), (1,)), ((), ()))


def phase_parts(frequencies, positions, period):
    product = frequencies[:, None] % period * positions[None, :] % period
    phases = np.float32(2.0 * np.pi / period) * product.astype(np.float32)
    return np.cos(phases), np.sin(phases)


def z_matrices():
    cosine, sine = phase_parts(np.arange(ZPW) - ZPW // 2, np.arange(NZ), NZ)
    full = np.zeros((ZPW, 2, NZ, 2), np.float32)
    full[:, 0, :, 0] = cosine
    full[:, 0, :, 1] = sine
    full[:, 1, :, 0] = -sine
    full[:, 1, :, 1] = cosine
    full = full.reshape(2 * ZPW, FFT, PLANES * 2).transpose(1, 2, 0)
    result = np.zeros((3, FFT, 8, 2, 2 * ZPW), np.float32)
    result[0, :, :, 0] = full[:, :8]
    result[1, :, :, 1] = full[:, :8]
    result[2, :, :4, 0] = full[:, 8:]
    result[2, :, 4:, 1] = full[:, 8:]
    return result.reshape(3 * FFT * 8, 4 * ZPW).astype(ml_dtypes.bfloat16)


def y_matrix():
    cosine, sine = phase_parts(np.arange(NY), np.arange(NY), NY)
    result = np.zeros((2, 128, 2, 128), np.float32)
    result[0, :NY, 0, :NY] = cosine
    result[0, :NY, 1, :NY] = sine
    result[1, :NY, 0, :NY] = -sine
    result[1, :NY, 1, :NY] = cosine
    return result.reshape(256, 256).astype(ml_dtypes.bfloat16)


def x_matrix():
    cosine, sine = phase_parts(np.arange(NX), np.arange(NX), NX)
    result = np.zeros((2, 2, 4, 2, 8, 2, NX), np.float32)
    for core in range(2):
        for chip in range(4):
            for high in range(2):
                owner = (high * 4 + chip) * 2 + core
                mine = slice(owner * 6, owner * 6 + 6)
                result[0, core, chip, high, :6, 0] = cosine[:, mine].T
                result[0, core, chip, high, :6, 1] = -sine[:, mine].T
                result[1, core, chip, high, :6, 0] = sine[:, mine].T
                result[1, core, chip, high, :6, 1] = cosine[:, mine].T
    return result.reshape(256, 2 * NX).astype(ml_dtypes.bfloat16)


def iota(shape, dim):
    return lax.broadcasted_iota(jnp.int32, shape, dim).astype(F32)


def onehot(condition):
    return jnp.where(condition, 1.0, 0.0).astype(BF16)


def dot(a, b):
    return jnp.dot(a, b, preferred_element_type=F32)


def dot_nt(a, b):
    return lax.dot_general(a, b, NT, preferred_element_type=F32)


def wait_bytes(ref, sem):
    pltpu.make_async_copy(ref, ref, sem).wait()


def kernel(
    coeff, col_map, eigen, band_ids, corners, z_mat, y_mat, x_mat, out,
    send, recv, own_levels, levels, weights, ranks, places, block_v, block_s,
    sorter, windows, columns, ordered, ordered_b, grid, field, density,
    terms, send_sem, recv_sem, local_sem, level_sem, sum_sem,
):
    fft = lax.axis_index("fft")
    pool = lax.axis_index("kpool")
    core = pool % 2
    chip = pool // 2 % 4
    high = pool // 8

    barrier = pltpu.get_barrier_semaphore()

    def greet_fft(step, carry):
        pl.semaphore_signal(
            barrier, inc=1, device_id={"fft": (fft + step) % FFT}, device_id_type=MESH
        )
        return carry

    def greet_pool(step, carry):
        pl.semaphore_signal(
            barrier, inc=1, device_id={"kpool": (pool + step) % POOLS}, device_id_type=MESH
        )
        return carry

    lax.fori_loop(1, FFT, greet_fft, 0)
    lax.fori_loop(1, POOLS, greet_pool, 0)

    def z_step(k):
        groups = []
        for pair in range(2):
            both = jnp.concatenate(
                [coeff[k, :, (2 * h + pair) * 384 : (2 * h + pair + 1) * 384] for h in range(2)],
                axis=0,
            )
            parts = dot_nt(z_mat[...], both).reshape(3, FFT, 8, 128)
            groups.extend(parts[part] for part in range(3))
        for tile in range(3):
            joined = jnp.concatenate([groups[2 * tile], groups[2 * tile + 1]], axis=1)
            send[k, :, 16 * tile : 16 * tile + 16, :] = joined.astype(BF16)

    def send_columns(k):
        def one(step, carry):
            target = (fft + step) % FFT
            pltpu.make_async_remote_copy(
                src_ref=send.at[k, target],
                dst_ref=recv.at[k, fft],
                send_sem=send_sem.at[k],
                recv_sem=recv_sem.at[k, fft // GROUP],
                device_id={"fft": target},
                device_id_type=MESH,
            ).start()
            return carry

        lax.fori_loop(1, FFT, one, 0)
        pltpu.make_async_copy(send.at[k, fft], recv.at[k, fft], local_sem.at[k]).start()

    z_step(0)
    pl.semaphore_wait(barrier, FFT - 1 + POOLS - 1)
    send_columns(0)

    band = lax.broadcasted_iota(jnp.int32, (BANDS, 2048), 0)
    chosen = jnp.zeros((BANDS, 2048), jnp.int32)
    for n in range(BANDS):
        chosen = jnp.where(band == n, band_ids[n], chosen)
    found = chosen == lax.broadcasted_iota(jnp.int32, (BANDS, 2048), 1)
    lane = lax.broadcasted_iota(jnp.int32, (BANDS, 128), 1)
    table = jnp.zeros((BANDS, 128), F32)
    for k in range(KP):
        picked = jnp.sum(jnp.where(found, eigen[k : k + 1, :], 0.0), axis=1, keepdims=True)
        table = jnp.where(lane == pool * KP + k, picked, table)
    own_levels[...] = table

    def send_levels(step, carry):
        pltpu.make_async_remote_copy(
            src_ref=own_levels,
            dst_ref=levels.at[pool],
            send_sem=level_sem.at[0],
            recv_sem=level_sem.at[1],
            device_id={"kpool": (pool + step) % POOLS},
            device_id_type=MESH,
        ).start()
        return carry

    lax.fori_loop(1, POOLS, send_levels, 0)
    pltpu.make_async_copy(own_levels, levels.at[pool], local_sem.at[2]).start()

    z_step(1)

    for k in range(KP):
        place = col_map[k : k + 1, :].astype(F32)
        x_of = jnp.floor((place + 0.5) * (1.0 / NY))
        y_of = place - NY * x_of
        rows = iota((128, COLS), 0)
        in_x_row = rows == x_of
        x_hot = onehot(in_x_row)
        y_hot = onehot(rows == y_of)
        taken = dot_nt(x_hot, y_hot)
        first = iota((128, 128), 0)
        second = iota((128, 128), 1)
        taken_b = taken.astype(BF16)
        before = dot(taken_b, onehot(first < second))
        above = dot(onehot(second < first), taken_b)
        start = jnp.sum(above, axis=1, keepdims=True)
        x_from = lax.broadcasted_iota(jnp.int32, (NX, COLS), 0) * NY
        count = jnp.sum(
            jnp.where(col_map[k : k + 1, :] < x_from, 1, 0), axis=1, keepdims=True
        )
        block_v[k] = jnp.broadcast_to(jnp.minimum(count >> 7, COLS // 128 - 1), (NX, 128))
        block = jnp.minimum(jnp.floor(start * (1.0 / 128)), COLS // 128 - 1.0)
        places[k] = jnp.where(taken > 0.5, start + before - 128.0 * block, -1.0).astype(jnp.int32)
        within = dot(before.astype(BF16), y_hot)
        rank = jnp.sum(jnp.where(in_x_row, start + within, 0.0), axis=0, keepdims=True)
        for group in range(GROUPS):
            ranks[k, group : group + 1, :] = rank[:, WIDE * group : WIDE * (group + 1)]
    block_copy = pltpu.make_async_copy(block_v, block_s, local_sem.at[3])
    block_copy.start()

    for k in range(KP):
        def sorter_rows(step, carry, k=k):
            group = step // 8
            part = step % 8
            rows = lax.broadcasted_iota(jnp.int32, (256, WIDE), 0) + part * 256
            sorter[
                k,
                pl.ds(pl.multiple_of(part * 256, 256), 256),
                pl.ds(pl.multiple_of(group * WIDE, WIDE), WIDE),
            ] = onehot(rows.astype(F32) == ranks[k, pl.ds(group, 1), :])
            return carry

        lax.fori_loop(0, GROUPS * 8, sorter_rows, 0)

        def window(step, carry, k=k):
            windows[k, step] = onehot(
                lax.broadcasted_iota(jnp.int32, (256, 128), 0)
                == places[k, pl.ds(2 * step + 1, 1), :]
            )
            return carry

        lax.fori_loop(0, NX // 2, window, 0)

    wait_bytes(send.at[0, pl.ds(0, FFT - 1)], send_sem.at[0])
    send_columns(1)

    def find_weights():
        wait_bytes(levels.at[pl.ds(0, POOLS - 1)], level_sem.at[1])
        pltpu.make_async_copy(own_levels, levels.at[pool], local_sem.at[2]).wait()
        every = levels[0]
        for j in range(1, POOLS):
            every = every + levels[j]
        kpoint = lax.broadcasted_iota(jnp.int32, (128, NTET), 0)
        member = jnp.zeros((128, NTET), F32)
        for c in range(4):
            member = member + jnp.where(corners[c : c + 1, :] == kpoint, 1.0, 0.0)
        mean = 0.25 * jnp.dot(
            every, member, precision=lax.Precision.HIGHEST, preferred_element_type=F32
        )
        occupied = jax.nn.sigmoid((0.0 - mean) / SMEARING)
        for k in range(KP):
            mine = jnp.zeros((1, NTET), F32)
            for c in range(4):
                mine = mine + jnp.where(corners[c : c + 1, :] == pool * KP + k, 1.0, 0.0)
            weight = jnp.sum(mine * occupied, axis=1, keepdims=True) * (2.0 / (4 * NTET))
            weights[k * BANDS : (k + 1) * BANDS, :] = jnp.broadcast_to(weight, (BANDS, 128))

    low = lax.broadcasted_iota(jnp.int32, (ROWS, 128), 1) < LOCAL

    def gather_group(k, group):
        upper, lower = [], []
        for pair in range(GROUP // 2):
            even = recv[k, GROUP * group + 2 * pair].astype(F32)
            odd = recv[k, GROUP * group + 2 * pair + 1].astype(F32)
            upper.append(jnp.where(low, even, pltpu.roll(odd, LOCAL, 1)))
            lower.append(jnp.where(low, pltpu.roll(even, LOCAL, 1), odd))
        return jnp.concatenate(
            [jnp.concatenate(upper, axis=1), jnp.concatenate(lower, axis=1)], axis=0
        ).astype(BF16)

    def each_group(k, work):
        def one(step, carry):
            group = (fft // GROUP + GROUPS - step) % GROUPS
            wait_bytes(recv.at[k, pl.ds(0, GROUP)], recv_sem.at[k, group])
            work(group)
            return carry

        lax.fori_loop(1, GROUPS, one, 0)
        group = fft // GROUP
        wait_bytes(recv.at[k, pl.ds(0, GROUP - 1)], recv_sem.at[k, group])
        pltpu.make_async_copy(send.at[k, fft], recv.at[k, fft], local_sem.at[k]).wait()
        work(group)

    def order_as_they_come(k):
        ordered[...] = jnp.zeros_like(ordered)

        def work(group):
            part_columns = gather_group(k, group)
            at = pl.ds(pl.multiple_of(group * WIDE, WIDE), WIDE)
            for part in range(8):
                moved = dot_nt(part_columns, sorter[k, 256 * part : 256 * (part + 1), at])
                ordered[2 * part] += moved[:, :128]
                ordered[2 * part + 1] += moved[:, 128:]

        each_group(k, work)

    def order_at_once(k):
        def work(group):
            columns[:, pl.ds(pl.multiple_of(group * WIDE, WIDE), WIDE)] = gather_group(k, group)

        each_group(k, work)

        def chunk(step, carry):
            at = pl.ds(pl.multiple_of(step * 256, 256), 256)
            moved = dot_nt(columns[...], sorter[k, at, :])
            ordered[2 * step] = moved[:, :128]
            ordered[2 * step + 1] = moved[:, 128:]
            return carry

        lax.fori_loop(0, COLS // 256, chunk, 0, unroll=2)

    def fill_grid(k):
        for block in range(COLS // 128 + 1):
            ordered_b[block] = ordered[block].astype(BF16)

        def two(step, carry):
            x = 2 * step
            block = block_s[k, x, 0]
            place = jnp.broadcast_to(places[k, pl.ds(x, 1), :], (2 * ROWS, 128))
            lane = place & 127
            near = jnp.take_along_axis(ordered[block], lane, axis=1, mode="promise_in_bounds")
            far = jnp.take_along_axis(ordered[block + 1], lane, axis=1, mode="promise_in_bounds")
            row = jnp.where(place < 0, 0.0, jnp.where(place < 128, near, far))
            grid[pl.ds(x * PITCH, 2 * ROWS), :] = row
            block = block_s[k, x + 1, 0]
            both = jnp.concatenate([ordered_b[block], ordered_b[block + 1]], axis=1)
            grid[pl.ds(x * PITCH + PITCH, 2 * ROWS), :] = dot(both, windows[k, step])
            return carry

        lax.fori_loop(0, NX // 2, two, 0, unroll=4)

    def add_plane(k, p):
        for pair in range(BANDS // 2):
            row = pair * 24 + (2 * p if p < 4 else 16 + 2 * (p - 4))
            apart = 8 if p < 4 else 4
            for e in range(2):
                for c in range(2):
                    field[(2 * pair + e) * NX : (2 * pair + e + 1) * NX, 128 * c : 128 * (c + 1)] = (
                        grid[pl.ds(row + apart * e + c, NX, stride=PITCH), :].astype(BF16)
                    )
        along_y = dot(field[...], y_mat[...]).astype(BF16)
        total = density[p]
        for pair in range(BANDS // 2):
            one, two = (
                along_y[(2 * pair + e) * NX : (2 * pair + e + 1) * NX] for e in range(2)
            )
            turned = jnp.concatenate(
                [
                    jnp.concatenate([one[:, :128], two[:, :128]], axis=1),
                    jnp.concatenate([one[:, 128:], two[:, 128:]], axis=1),
                ],
                axis=0,
            )
            psi = dot(x_mat[...], turned)
            power = psi[:128] * psi[:128] + psi[128:] * psi[128:]
            at = k * BANDS + 2 * pair
            total = total + (
                weights[at : at + 1, :] * power[:, :128]
                + weights[at + 1 : at + 2, :] * power[:, 128:]
            )
        density[p] = total

    def planes(batch):
        return pl.ds(BATCH * batch, BATCH)

    def rows_of(owner):
        place = (owner % 2) * 8 + (owner // 2 % 4) * 2 + owner // 8
        return pl.ds(pl.multiple_of(place * 8, 8), OWNED)

    def term_copies(batch):
        copies = []
        for step in range(1, POOLS):
            turn = POOLS - step
            owner = ((high + turn // 8) % 2) * 8 + (chip * 2 + core + turn) % 8
            copies.append(
                pltpu.make_async_remote_copy(
                    src_ref=density.at[planes(batch), rows_of(owner), :],
                    dst_ref=terms.at[step - 1, planes(batch)],
                    send_sem=sum_sem.at[0, batch],
                    recv_sem=sum_sem.at[1, batch],
                    device_id={"kpool": owner},
                    device_id_type=MESH,
                )
            )
        return copies

    def sum_terms(batch):
        at = planes(batch)
        wait_bytes(terms.at[:, at], sum_sem.at[1, batch])
        total = density[at, rows_of(pool), :]
        for step in range(POOLS - 1):
            total = total + terms[step, at]
        for i in range(6):
            out[BATCH * batch : BATCH * (batch + 1), NY * i : NY * (i + 1)] = total[:, i, :NY]

    density[...] = jnp.zeros_like(density)
    block_copy.wait()

    order_as_they_come(0)
    find_weights()
    fill_grid(0)
    for p in range(PLANES):
        add_plane(0, p)
    order_at_once(1)
    fill_grid(1)
    for batch in range(BATCHES):
        for p in range(BATCH):
            add_plane(1, BATCH * batch + p)
        for copy in term_copies(batch):
            copy.start()
    for batch in range(BATCHES):
        sum_terms(batch)

    for batch in range(BATCHES):
        wait_bytes(terms.at[:, planes(batch)], sum_sem.at[0, batch])
    wait_bytes(send.at[1, pl.ds(0, FFT - 1)], send_sem.at[1])
    wait_bytes(levels.at[pl.ds(0, POOLS - 1)], level_sem.at[0])


def per_device(coeff, col_map, eigen, band_ids, tet_corners):
    vmem = pl.BlockSpec(memory_space=pltpu.VMEM)
    smem = pl.BlockSpec(memory_space=pltpu.SMEM)
    return pl.pallas_call(
        kernel,
        out_shape=jax.ShapeDtypeStruct((PLANES, 6 * NY), F32),
        in_specs=[vmem, vmem, vmem, smem, vmem, vmem, vmem, vmem],
        out_specs=vmem,
        scratch_shapes=[
            pltpu.VMEM((KP, FFT, ROWS, 128), BF16),
            pltpu.VMEM((KP, FFT, ROWS, 128), BF16),
            pltpu.VMEM((8, 128), F32),
            pltpu.VMEM((POOLS, 8, 128), F32),
            pltpu.VMEM((KP * BANDS, 128), F32),
            pltpu.VMEM((KP, GROUPS, WIDE), F32),
            pltpu.VMEM((KP, 128, 128), jnp.int32),
            pltpu.VMEM((KP, NX, 128), jnp.int32),
            pltpu.SMEM((KP, NX, 128), jnp.int32),
            pltpu.VMEM((KP, COLS, COLS), BF16),
            pltpu.VMEM((KP, NX // 2, 256, 128), BF16),
            pltpu.VMEM((2 * ROWS, COLS), BF16),
            pltpu.VMEM((COLS // 128 + 1, 2 * ROWS, 128), F32),
            pltpu.VMEM((COLS // 128 + 1, 2 * ROWS, 128), BF16),
            pltpu.VMEM((NX * PITCH, 128), F32),
            pltpu.VMEM((BANDS * NX, 256), BF16),
            pltpu.VMEM((PLANES, 128, 128), F32),
            pltpu.VMEM((POOLS - 1, PLANES, OWNED, 128), F32),
            pltpu.SemaphoreType.DMA((KP,)),
            pltpu.SemaphoreType.DMA((KP, GROUPS)),
            pltpu.SemaphoreType.DMA((4,)),
            pltpu.SemaphoreType.DMA((2,)),
            pltpu.SemaphoreType.DMA((2, BATCHES)),
        ],
        compiler_params=pltpu.CompilerParams(
            collective_id=0, has_side_effects=True, vmem_limit_bytes=56 * 1024 * 1024
        ),
    )(
        coeff, col_map, eigen, band_ids, tet_corners.T,
        jnp.asarray(z_matrices()), jnp.asarray(y_matrix()), jnp.asarray(x_matrix()),
    )


def solution(mesh):
    in_specs = (P("kpool", "fft", None), P("kpool", None), P("kpool", None), P(), P())
    out_specs = P("fft", "kpool")
    return jax.shard_map(
        per_device, mesh=mesh, in_specs=in_specs, out_specs=out_specs, check_vma=False
    )
```

```python
import functools

import jax
import jax.numpy as jnp
import ml_dtypes
import numpy as np
from jax import lax
from jax.experimental import pallas as pl
from jax.experimental.pallas import tpu as pltpu
from jax.sharding import PartitionSpec as P

NX = 96
NY = 96
NZ = 192
ZPW = 96
BANDS = 8
COLS = 2048
KPOINTS = 32
NTET = 192

FFT = 32
POOLS = 16
KP = 2
LOCAL = COLS // FFT
PLANES = NZ // FFT
ROWS = 48
GROUP = 4
GROUPS = FFT // GROUP
WIDE = GROUP * LOCAL
PITCH = 2 * ROWS + 8
BATCH = 2
OWNED = 6
BATCHES = PLANES // BATCH
SMEARING = 0.1
MESH = pl.DeviceIdType.MESH
F32 = jnp.float32
BF16 = jnp.bfloat16
NT = (((1,), (1,)), ((), ()))


def phase_parts(frequencies, positions, period):
    product = frequencies[:, None] % period * positions[None, :] % period
    phases = np.float32(2.0 * np.pi / period) * product.astype(np.float32)
    return np.cos(phases), np.sin(phases)


def z_matrices():
    cosine, sine = phase_parts(np.arange(ZPW) - ZPW // 2, np.arange(NZ), NZ)
    full = np.zeros((ZPW, 2, NZ, 2), np.float32)
    full[:, 0, :, 0] = cosine
    full[:, 0, :, 1] = sine
    full[:, 1, :, 0] = -sine
    full[:, 1, :, 1] = cosine
    full = full.reshape(2 * ZPW, FFT, PLANES * 2).transpose(1, 2, 0)
    result = np.zeros((3, FFT, 8, 2, 2 * ZPW), np.float32)
    result[0, :, :, 0] = full[:, :8]
    result[1, :, :, 1] = full[:, :8]
    result[2, :, :4, 0] = full[:, 8:]
    result[2, :, 4:, 1] = full[:, 8:]
    return result.reshape(3 * FFT * 8, 4 * ZPW).astype(ml_dtypes.bfloat16)


def y_matrix():
    cosine, sine = phase_parts(np.arange(NY), np.arange(NY), NY)
    result = np.zeros((2, 128, 2, 128), np.float32)
    result[0, :NY, 0, :NY] = cosine
    result[0, :NY, 1, :NY] = sine
    result[1, :NY, 0, :NY] = -sine
    result[1, :NY, 1, :NY] = cosine
    return result.reshape(256, 256).astype(ml_dtypes.bfloat16)


def x_matrix():
    cosine, sine = phase_parts(np.arange(NX), np.arange(NX), NX)
    result = np.zeros((2, 2, 4, 2, 8, 2, NX), np.float32)
    for core in range(2):
        for chip in range(4):
            for high in range(2):
                owner = (high * 4 + chip) * 2 + core
                mine = slice(owner * 6, owner * 6 + 6)
                result[0, core, chip, high, :6, 0] = cosine[:, mine].T
                result[0, core, chip, high, :6, 1] = -sine[:, mine].T
                result[1, core, chip, high, :6, 0] = sine[:, mine].T
                result[1, core, chip, high, :6, 1] = cosine[:, mine].T
    return result.reshape(256, 2 * NX).astype(ml_dtypes.bfloat16)


def iota(shape, dim):
    return lax.broadcasted_iota(jnp.int32, shape, dim).astype(F32)


def onehot(condition):
    return jnp.where(condition, 1.0, 0.0).astype(BF16)


def dot(a, b):
    return jnp.dot(a, b, preferred_element_type=F32)


def dot_nt(a, b):
    return lax.dot_general(a, b, NT, preferred_element_type=F32)


def wait_bytes(ref, sem):
    pltpu.make_async_copy(ref, ref, sem).wait()


def kernel(
    coeff, col_map, eigen, band_ids, corners, z_mat, y_mat, x_mat, out,
    send, recv, own_levels, levels, weights, ranks, places, block_v, block_s,
    sorter, windows, columns, ordered, ordered_b, grid, field, density,
    terms, send_sem, recv_sem, local_sem, level_sem, sum_sem,
):
    fft = lax.axis_index("fft")
    pool = lax.axis_index("kpool")
    core = pool % 2
    chip = pool // 2 % 4
    high = pool // 8

    barrier = pltpu.get_barrier_semaphore()

    def greet_fft(step, carry):
        pl.semaphore_signal(
            barrier, inc=1, device_id={"fft": (fft + step) % FFT}, device_id_type=MESH
        )
        return carry

    def greet_pool(step, carry):
        pl.semaphore_signal(
            barrier, inc=1, device_id={"kpool": (pool + step) % POOLS}, device_id_type=MESH
        )
        return carry

    lax.fori_loop(1, FFT, greet_fft, 0)
    lax.fori_loop(1, POOLS, greet_pool, 0)

    def z_step(k):
        groups = []
        for pair in range(2):
            both = jnp.concatenate(
                [coeff[k, :, (2 * h + pair) * 384 : (2 * h + pair + 1) * 384] for h in range(2)],
                axis=0,
            )
            parts = dot_nt(z_mat[...], both).reshape(3, FFT, 8, 128)
            groups.extend(parts[part] for part in range(3))
        for tile in range(3):
            joined = jnp.concatenate([groups[2 * tile], groups[2 * tile + 1]], axis=1)
            send[k, :, 16 * tile : 16 * tile + 16, :] = joined.astype(BF16)

    def send_columns(k):
        def one(step, carry):
            target = (fft + step) % FFT
            pltpu.make_async_remote_copy(
                src_ref=send.at[k, target],
                dst_ref=recv.at[k, fft],
                send_sem=send_sem.at[k],
                recv_sem=recv_sem.at[k, fft // GROUP],
                device_id={"fft": target},
                device_id_type=MESH,
            ).start()
            return carry

        lax.fori_loop(1, FFT, one, 0)
        pltpu.make_async_copy(send.at[k, fft], recv.at[k, fft], local_sem.at[k]).start()

    z_step(0)
    pl.semaphore_wait(barrier, FFT - 1 + POOLS - 1)
    send_columns(0)

    band = lax.broadcasted_iota(jnp.int32, (BANDS, 2048), 0)
    chosen = jnp.zeros((BANDS, 2048), jnp.int32)
    for n in range(BANDS):
        chosen = jnp.where(band == n, band_ids[n], chosen)
    found = chosen == lax.broadcasted_iota(jnp.int32, (BANDS, 2048), 1)
    lane = lax.broadcasted_iota(jnp.int32, (BANDS, 128), 1)
    table = jnp.zeros((BANDS, 128), F32)
    for k in range(KP):
        picked = jnp.sum(jnp.where(found, eigen[k : k + 1, :], 0.0), axis=1, keepdims=True)
        table = jnp.where(lane == pool * KP + k, picked, table)
    own_levels[...] = table

    def send_levels(step, carry):
        pltpu.make_async_remote_copy(
            src_ref=own_levels,
            dst_ref=levels.at[pool],
            send_sem=level_sem.at[0],
            recv_sem=level_sem.at[1],
            device_id={"kpool": (pool + step) % POOLS},
            device_id_type=MESH,
        ).start()
        return carry

    lax.fori_loop(1, POOLS, send_levels, 0)
    pltpu.make_async_copy(own_levels, levels.at[pool], local_sem.at[2]).start()

    z_step(1)

    for k in range(KP):
        place = col_map[k : k + 1, :].astype(F32)
        x_of = jnp.floor((place + 0.5) * (1.0 / NY))
        y_of = place - NY * x_of
        rows = iota((128, COLS), 0)
        in_x_row = rows == x_of
        x_hot = onehot(in_x_row)
        y_hot = onehot(rows == y_of)
        taken = dot_nt(x_hot, y_hot)
        first = iota((128, 128), 0)
        second = iota((128, 128), 1)
        taken_b = taken.astype(BF16)
        before = dot(taken_b, onehot(first < second))
        above = dot(onehot(second < first), taken_b)
        start = jnp.sum(above, axis=1, keepdims=True)
        x_from = lax.broadcasted_iota(jnp.int32, (NX, COLS), 0) * NY
        count = jnp.sum(
            jnp.where(col_map[k : k + 1, :] < x_from, 1, 0), axis=1, keepdims=True
        )
        block_v[k] = jnp.broadcast_to(jnp.minimum(count >> 7, COLS // 128 - 1), (NX, 128))
        block = jnp.minimum(jnp.floor(start * (1.0 / 128)), COLS // 128 - 1.0)
        places[k] = jnp.where(taken > 0.5, start + before - 128.0 * block, -1.0).astype(jnp.int32)
        within = dot(before.astype(BF16), y_hot)
        rank = jnp.sum(jnp.where(in_x_row, start + within, 0.0), axis=0, keepdims=True)
        for group in range(GROUPS):
            ranks[k, group : group + 1, :] = rank[:, WIDE * group : WIDE * (group + 1)]
    block_copy = pltpu.make_async_copy(block_v, block_s, local_sem.at[3])
    block_copy.start()

    for k in range(KP):
        def sorter_rows(step, carry, k=k):
            group = step // 8
            part = step % 8
            rows = lax.broadcasted_iota(jnp.int32, (256, WIDE), 0) + part * 256
            sorter[
                k,
                pl.ds(pl.multiple_of(part * 256, 256), 256),
                pl.ds(pl.multiple_of(group * WIDE, WIDE), WIDE),
            ] = onehot(rows.astype(F32) == ranks[k, pl.ds(group, 1), :])
            return carry

        lax.fori_loop(0, GROUPS * 8, sorter_rows, 0)

        def window(step, carry, k=k):
            windows[k, step] = onehot(
                lax.broadcasted_iota(jnp.int32, (256, 128), 0)
                == places[k, pl.ds(2 * step + 1, 1), :]
            )
            return carry

        lax.fori_loop(0, NX // 2, window, 0)

    send_columns(1)

    def find_weights():
        wait_bytes(levels.at[pl.ds(0, POOLS - 1)], level_sem.at[1])
        pltpu.make_async_copy(own_levels, levels.at[pool], local_sem.at[2]).wait()
        every = levels[0]
        for j in range(1, POOLS):
            every = every + levels[j]
        kpoint = lax.broadcasted_iota(jnp.int32, (128, NTET), 0)
        member = jnp.zeros((128, NTET), F32)
        for c in range(4):
            member = member + jnp.where(corners[c : c + 1, :] == kpoint, 1.0, 0.0)
        mean = 0.25 * jnp.dot(
            every, member, precision=lax.Precision.HIGHEST, preferred_element_type=F32
        )
        occupied = jax.nn.sigmoid((0.0 - mean) / SMEARING)
        for k in range(KP):
            mine = jnp.zeros((1, NTET), F32)
            for c in range(4):
                mine = mine + jnp.where(corners[c : c + 1, :] == pool * KP + k, 1.0, 0.0)
            weight = jnp.sum(mine * occupied, axis=1, keepdims=True) * (2.0 / (4 * NTET))
            weights[k * BANDS : (k + 1) * BANDS, :] = jnp.broadcast_to(weight, (BANDS, 128))

    low = lax.broadcasted_iota(jnp.int32, (ROWS, 128), 1) < LOCAL

    def gather_group(k, group):
        upper, lower = [], []
        for pair in range(GROUP // 2):
            even = recv[k, GROUP * group + 2 * pair].astype(F32)
            odd = recv[k, GROUP * group + 2 * pair + 1].astype(F32)
            upper.append(jnp.where(low, even, pltpu.roll(odd, LOCAL, 1)))
            lower.append(jnp.where(low, pltpu.roll(even, LOCAL, 1), odd))
        return jnp.concatenate(
            [jnp.concatenate(upper, axis=1), jnp.concatenate(lower, axis=1)], axis=0
        ).astype(BF16)

    def each_group(k, work):
        def one(step, carry):
            group = (fft // GROUP + GROUPS - step) % GROUPS
            wait_bytes(recv.at[k, pl.ds(0, GROUP)], recv_sem.at[k, group])
            work(group)
            return carry

        lax.fori_loop(1, GROUPS, one, 0)
        group = fft // GROUP
        wait_bytes(recv.at[k, pl.ds(0, GROUP - 1)], recv_sem.at[k, group])
        pltpu.make_async_copy(send.at[k, fft], recv.at[k, fft], local_sem.at[k]).wait()
        work(group)

    def order_as_they_come(k):
        ordered[...] = jnp.zeros_like(ordered)

        def work(group):
            part_columns = gather_group(k, group)
            at = pl.ds(pl.multiple_of(group * WIDE, WIDE), WIDE)
            for part in range(8):
                moved = dot_nt(part_columns, sorter[k, 256 * part : 256 * (part + 1), at])
                ordered[2 * part] += moved[:, :128]
                ordered[2 * part + 1] += moved[:, 128:]

        each_group(k, work)

    def order_at_once(k):
        def work(group):
            columns[:, pl.ds(pl.multiple_of(group * WIDE, WIDE), WIDE)] = gather_group(k, group)

        each_group(k, work)

        def chunk(step, carry):
            at = pl.ds(pl.multiple_of(step * 256, 256), 256)
            moved = dot_nt(columns[...], sorter[k, at, :])
            ordered[2 * step] = moved[:, :128]
            ordered[2 * step + 1] = moved[:, 128:]
            return carry

        lax.fori_loop(0, COLS // 256, chunk, 0, unroll=2)

    def fill_grid(k):
        for block in range(COLS // 128 + 1):
            ordered_b[block] = ordered[block].astype(BF16)

        def two(step, carry):
            x = 2 * step
            block = block_s[k, x, 0]
            place = jnp.broadcast_to(places[k, pl.ds(x, 1), :], (2 * ROWS, 128))
            lane = place & 127
            near = jnp.take_along_axis(ordered[block], lane, axis=1, mode="promise_in_bounds")
            far = jnp.take_along_axis(ordered[block + 1], lane, axis=1, mode="promise_in_bounds")
            row = jnp.where(place < 0, 0.0, jnp.where(place < 128, near, far))
            grid[pl.ds(x * PITCH, 2 * ROWS), :] = row
            block = block_s[k, x + 1, 0]
            both = jnp.concatenate([ordered_b[block], ordered_b[block + 1]], axis=1)
            grid[pl.ds(x * PITCH + PITCH, 2 * ROWS), :] = dot(both, windows[k, step])
            return carry

        lax.fori_loop(0, NX // 2, two, 0, unroll=4)

    def add_plane(k, p):
        for pair in range(BANDS // 2):
            row = pair * 24 + (2 * p if p < 4 else 16 + 2 * (p - 4))
            apart = 8 if p < 4 else 4
            for e in range(2):
                for c in range(2):
                    field[(2 * pair + e) * NX : (2 * pair + e + 1) * NX, 128 * c : 128 * (c + 1)] = (
                        grid[pl.ds(row + apart * e + c, NX, stride=PITCH), :].astype(BF16)
                    )
        along_y = dot(field[...], y_mat[...]).astype(BF16)
        total = density[p]
        for pair in range(BANDS // 2):
            one, two = (
                along_y[(2 * pair + e) * NX : (2 * pair + e + 1) * NX] for e in range(2)
            )
            turned = jnp.concatenate(
                [
                    jnp.concatenate([one[:, :128], two[:, :128]], axis=1),
                    jnp.concatenate([one[:, 128:], two[:, 128:]], axis=1),
                ],
                axis=0,
            )
            psi = dot(x_mat[...], turned)
            power = psi[:128] * psi[:128] + psi[128:] * psi[128:]
            at = k * BANDS + 2 * pair
            total = total + (
                weights[at : at + 1, :] * power[:, :128]
                + weights[at + 1 : at + 2, :] * power[:, 128:]
            )
        density[p] = total

    def planes(batch):
        return pl.ds(BATCH * batch, BATCH)

    def rows_of(owner):
        place = (owner % 2) * 8 + (owner // 2 % 4) * 2 + owner // 8
        return pl.ds(pl.multiple_of(place * 8, 8), OWNED)

    def term_copies(batch):
        copies = []
        for step in range(1, POOLS):
            turn = POOLS - step
            owner = ((high + turn // 8) % 2) * 8 + (chip * 2 + core + turn) % 8
            copies.append(
                pltpu.make_async_remote_copy(
                    src_ref=density.at[planes(batch), rows_of(owner), :],
                    dst_ref=terms.at[step - 1, planes(batch)],
                    send_sem=sum_sem.at[0, batch],
                    recv_sem=sum_sem.at[1, batch],
                    device_id={"kpool": owner},
                    device_id_type=MESH,
                )
            )
        return copies

    def sum_terms(batch):
        at = planes(batch)
        wait_bytes(terms.at[:, at], sum_sem.at[1, batch])
        total = density[at, rows_of(pool), :]
        for step in range(POOLS - 1):
            total = total + terms[step, at]
        for i in range(6):
            out[BATCH * batch : BATCH * (batch + 1), NY * i : NY * (i + 1)] = total[:, i, :NY]

    density[...] = jnp.zeros_like(density)
    block_copy.wait()

    order_as_they_come(0)
    find_weights()
    fill_grid(0)
    for p in range(PLANES):
        add_plane(0, p)
    order_at_once(1)
    fill_grid(1)
    for batch in range(BATCHES):
        for p in range(BATCH):
            add_plane(1, BATCH * batch + p)
        for copy in term_copies(batch):
            copy.start()
    for batch in range(BATCHES):
        sum_terms(batch)

    for batch in range(BATCHES):
        wait_bytes(terms.at[:, planes(batch)], sum_sem.at[0, batch])
    for k in range(KP):
        wait_bytes(send.at[k, pl.ds(0, FFT - 1)], send_sem.at[k])
    wait_bytes(levels.at[pl.ds(0, POOLS - 1)], level_sem.at[0])


def per_device(coeff, col_map, eigen, band_ids, tet_corners):
    vmem = pl.BlockSpec(memory_space=pltpu.VMEM)
    smem = pl.BlockSpec(memory_space=pltpu.SMEM)
    return pl.pallas_call(
        kernel,
        out_shape=jax.ShapeDtypeStruct((PLANES, 6 * NY), F32),
        in_specs=[vmem, vmem, vmem, smem, vmem, vmem, vmem, vmem],
        out_specs=vmem,
        scratch_shapes=[
            pltpu.VMEM((KP, FFT, ROWS, 128), BF16),
            pltpu.VMEM((KP, FFT, ROWS, 128), BF16),
            pltpu.VMEM((8, 128), F32),
            pltpu.VMEM((POOLS, 8, 128), F32),
            pltpu.VMEM((KP * BANDS, 128), F32),
            pltpu.VMEM((KP, GROUPS, WIDE), F32),
            pltpu.VMEM((KP, 128, 128), jnp.int32),
            pltpu.VMEM((KP, NX, 128), jnp.int32),
            pltpu.SMEM((KP, NX, 128), jnp.int32),
            pltpu.VMEM((KP, COLS, COLS), BF16),
            pltpu.VMEM((KP, NX // 2, 256, 128), BF16),
            pltpu.VMEM((2 * ROWS, COLS), BF16),
            pltpu.VMEM((COLS // 128 + 1, 2 * ROWS, 128), F32),
            pltpu.VMEM((COLS // 128 + 1, 2 * ROWS, 128), BF16),
            pltpu.VMEM((NX * PITCH, 128), F32),
            pltpu.VMEM((BANDS * NX, 256), BF16),
            pltpu.VMEM((PLANES, 128, 128), F32),
            pltpu.VMEM((POOLS - 1, PLANES, OWNED, 128), F32),
            pltpu.SemaphoreType.DMA((KP,)),
            pltpu.SemaphoreType.DMA((KP, GROUPS)),
            pltpu.SemaphoreType.DMA((4,)),
            pltpu.SemaphoreType.DMA((2,)),
            pltpu.SemaphoreType.DMA((2, BATCHES)),
        ],
        compiler_params=pltpu.CompilerParams(
            collective_id=0, has_side_effects=True, vmem_limit_bytes=56 * 1024 * 1024
        ),
    )(
        coeff, col_map, eigen, band_ids, tet_corners.T,
        jnp.asarray(z_matrices()), jnp.asarray(y_matrix()), jnp.asarray(x_matrix()),
    )


def solution(mesh):
    in_specs = (P("kpool", "fft", None), P("kpool", None), P("kpool", None), P(), P())
    out_specs = P("fft", "kpool")
    return jax.shard_map(
        per_device, mesh=mesh, in_specs=in_specs, out_specs=out_specs, check_vma=False
    )
```
